32 devices in a mesh: dp: 2 (over x), node: 2 (over core), local: 8 (over z, y).
Axes of the slice: x: 2, y: 2, z: 4, core: 2. Of those that a mesh axis runs over, the one named last changes fastest.
Arguments:
- tokens: bfloat16 [4096, 2048], P(('dp', 'node', 'local')), may hold values from -6 to 6
- cotangent: bfloat16 [4096, 2048], P(('dp', 'node', 'local')), may hold values from -4 to 4
- routes: int32 [4096, 8], P(('dp', 'node', 'local')), may hold values from 0 to 15, all different within a row; in each aligned block of 128 rows (0 to 127, 128 to 255, ...) at most 96 rows name the same one
- gates: bfloat16 [4096, 8], P(('dp', 'node', 'local')), may hold values from 0.029907227 to 0.3984375
- w_gate: bfloat16 [16, 2048, 384], P(('node', 'local'), 'dp'), may hold values from -0.125 to 0.125
- w_up: bfloat16 [16, 2048, 384], P(('node', 'local'), 'dp'), may hold values from -0.125 to 0.125
- w_down: bfloat16 [16, 2048, 384], P(('node', 'local'), 'dp'), may hold values from -0.3125 to 0.3125
Outputs:
- input_grad: bfloat16 [4096, 2048], P(('dp', 'node', 'local'))
- gate_grad: bfloat16 [4096, 8], P(('dp', 'node', 'local'))
- gate_weight_grad: float32 [16, 2048, 384], P(('node', 'local'), 'dp')
- up_weight_grad: float32 [16, 2048, 384], P(('node', 'local'), 'dp')
- down_weight_grad: float32 [16, 2048, 384], P(('node', 'local'), 'dp')
The draws below stay inside these ranges and needn't reach their ends.
Inputs may be any that keep to these rules, and one draw needn't show every extreme that they name: `routes`: each token names 8 different experts. Among the tokens of one device no expert is named more than 96 times, and on some device some expert is named exactly 96 times.
All inputs are finite; a program needn't handle non-finite values.
Results may differ from the reference program's by a relative error of at most 0.0057.
Values may be sent and summed in bfloat16 or wider, within the bound.
A program may use at most 128 MiB of HBM per device.

```python
import math
import jax
import jax.numpy as jnp
import numpy as np
from jax import lax

D = 2048
FF = 384
TOP = 8
TOK_DEV = 128
EXPERTS = 16
CAP = 96
TOKENS = 4096
N_DP = 2
N_NODE = 2
N_LOCAL = 8


def levels(rng, extent, cuts, low, top_value):
    gain, own = 1.0, jax.random.fold_in(rng, 6)
    for axis_at, shards_of in cuts:
        heights = jnp.exp(jax.random.uniform(jax.random.fold_in(own, axis_at), (shards_of,), jnp.float32, low / len(cuts), top_value / len(cuts)))
        gain = gain * jnp.repeat(heights, extent[axis_at] // shards_of).reshape([-1 if axis == axis_at else 1 for axis in range(len(extent))])
    return gain


def assign_block(key, own, number, rows, amount, top, limit, lean):
    sequence = jax.random.permutation(key, amount)
    crowded, usual = load_shares(amount, rows * top, limit, lean, True), load_shares(amount, rows * top, limit, lean, False)
    places = jnp.arange(amount)

    def named(tallies, turn):
        used = int((tallies > 0).sum())
        fixed = max(1, used // 4)
        shifted = fixed + (places - fixed + turn * (used - fixed)) % max(1, amount - fixed)
        return jnp.zeros((amount,), jnp.int32).at[sequence[jnp.where(places < fixed, places, shifted)]].set(jnp.asarray(tallies, jnp.int32))

    tallies = jnp.where(number % 4 == 0, named(crowded, number // 4), named(usual, number - number // 4 - 1))
    mixed = jax.random.permutation(jax.random.fold_in(own, 3), amount)
    donor, receiver = mixed[0:amount // 2 * 2:2], mixed[1:amount // 2 * 2:2]
    slack = jnp.minimum(tallies[donor] - 1, limit - tallies[receiver]) // 2
    slack = jnp.where((donor == sequence[0]) | (receiver == sequence[0]) | (tallies[receiver] == 0), 0, jnp.maximum(slack, 0))
    shifted = jax.random.randint(jax.random.fold_in(own, 4), (amount // 2,), 0, 1 << 20) % (slack + 1)
    tallies = tallies.at[donor].add(-shifted).at[receiver].add(shifted)
    members = jnp.searchsorted(jnp.cumsum(tallies), jnp.arange(rows * top), side="right").astype(jnp.int32)
    listing = members.reshape(top, rows).T
    listing = listing[jax.random.permutation(jax.random.fold_in(own, 1), rows)]
    turn = jax.random.randint(jax.random.fold_in(own, 2), (rows, 1), 0, top)
    return jnp.take_along_axis(listing, (jnp.arange(top)[None, :] + turn) % top, axis=1)


def load_shares(amount, total, bound, lean, full):
    weights = [(1 << 20) // math.isqrt(standing ** lean) + 1 for standing in range(1, amount + 1)]
    largest = bound if full else min(bound, max(-(-total // amount), total * weights[0] // sum(weights)))
    least = 1 if total - largest >= amount - 1 else 0
    holding, rest = [largest] + [least] * (amount - 1), total - largest - least * (amount - 1)
    while rest > 0:
        movable = [i for i in range(1, amount) if holding[i] < largest] or [i for i in range(1, amount) if holding[i] < bound]
        pool, budget = sum([weights[i] for i in movable]), rest
        for i in movable:
            extra = min(bound - holding[i], max(1, budget * weights[i] // pool), rest)
            holding[i] = holding[i] + extra
            rest = rest - extra
    return np.array(holding)


def centred(own_key, dims, scale, reach, pieces=(), kind=jnp.bfloat16):
    array = jax.random.normal(own_key, dims, jnp.float32) * scale
    if len(pieces) > 0:
        array = levels(own_key, dims, pieces, -0.22, 0.18) * array
    return jnp.clip(array, min=-reach, max=reach).astype(kind)


def setup_inputs(seed: int = 0) -> dict:
    streams_of = jax.random.split(jax.random.key(seed), 8)
    tokens = centred(streams_of[0], (TOKENS, D), 1.0, 6.0, ((0, 32),))
    cotangent = centred(streams_of[1], (TOKENS, D), 0.5, 4.0, ((0, 32),))
    routes_keys = jax.random.split(jax.random.fold_in(streams_of[2], 1), TOKENS // TOK_DEV)
    routes_turns = jax.random.permutation(jax.random.fold_in(streams_of[2], 3), TOKENS // TOK_DEV)
    routes = jax.vmap(lambda own, number: assign_block(jax.random.fold_in(streams_of[2], 2), own, number, TOK_DEV, EXPERTS, TOP, CAP, 2))(routes_keys, routes_turns).reshape((TOKENS, TOP))
    gates = jnp.clip(jnp.exp(math.log(0.3984375) - 2.5894505 * jax.random.uniform(streams_of[3], (TOKENS, TOP), jnp.float32) ** levels(streams_of[3], (TOKENS, TOP), ((0, 32),), -0.2, 0.2)), 0.029907227, 0.3984375).astype(jnp.bfloat16)
    w_gate = centred(streams_of[4], (EXPERTS, D, FF), D ** -0.5, 0.125, ((0, 16), (1, 2)))
    w_up = centred(streams_of[5], (EXPERTS, D, FF), D ** -0.5, 0.125, ((0, 16), (1, 2)))
    w_down = centred(streams_of[6], (EXPERTS, D, FF), FF ** -0.5, 0.3125, ((0, 16), (1, 2)))
    return dict(tokens=tokens, cotangent=cotangent, routes=routes, gates=gates, w_gate=w_gate, w_up=w_up, w_down=w_down)


def expert_rows(rows_x, rows_dy, rows_gate, gate_proj, up_proj, down_proj):
    pre_gate = jnp.dot(rows_x, gate_proj, preferred_element_type=jnp.float32)
    pre_up = jnp.dot(rows_x, up_proj, preferred_element_type=jnp.float32)
    gate_sigmoid = jax.nn.sigmoid(pre_gate)
    activated = pre_gate * gate_sigmoid
    hidden = activated * pre_up
    upstream = jnp.dot(rows_dy, down_proj, preferred_element_type=jnp.float32)
    gate_grad = jnp.sum(upstream * hidden, axis=1).astype(jnp.bfloat16)
    weight = rows_gate.astype(jnp.float32)[:, None]
    scaled_hidden = (weight * hidden).astype(jnp.bfloat16)
    hidden_grad = weight * upstream
    pre_gate_grad = (hidden_grad * pre_up * gate_sigmoid * (1.0 + pre_gate * (1.0 - gate_sigmoid))).astype(jnp.bfloat16)
    pre_up_grad = (hidden_grad * activated).astype(jnp.bfloat16)
    over_rows = (((0,), (0,)), ((), ()))
    down_grad = lax.dot_general(rows_dy, scaled_hidden, over_rows, preferred_element_type=jnp.float32)
    gate_wgrad = lax.dot_general(rows_x, pre_gate_grad, over_rows, preferred_element_type=jnp.float32)
    up_wgrad = lax.dot_general(rows_x, pre_up_grad, over_rows, preferred_element_type=jnp.float32)
    over_hidden = (((1,), (1,)), ((), ()))
    input_rows = lax.dot_general(pre_gate_grad, gate_proj, over_hidden, preferred_element_type=jnp.float32)
    input_rows = input_rows + lax.dot_general(pre_up_grad, up_proj, over_hidden, preferred_element_type=jnp.float32)
    return input_rows.astype(jnp.bfloat16), gate_grad, gate_wgrad, up_wgrad, down_grad


def reference(tokens, cotangent, routes, gates, w_gate, w_up, w_down):
    pick_count = TOKENS * TOP
    flat_routes = routes.reshape(pick_count)
    flat_gates = gates.reshape(pick_count)
    sorted_picks = jnp.argsort(flat_routes, stable=True).astype(jnp.int32)
    expert_ids = jnp.arange(EXPERTS, dtype=jnp.int32)
    counts = jnp.sum((flat_routes[:, None] == expert_ids[None, :]).astype(jnp.int32), axis=0)
    starts = (jnp.cumsum(counts) - counts).astype(jnp.int32)
    most_rows = CAP * N_DP * N_NODE * N_LOCAL
    picks_ext = jnp.concatenate([sorted_picks, jnp.zeros((most_rows,), jnp.int32)])

    def one_expert(running, expert):
        input_total, gate_total = running
        chosen = lax.dynamic_slice_in_dim(picks_ext, starts[expert], most_rows)
        is_valid = jnp.arange(most_rows, dtype=jnp.int32) < counts[expert]
        owner_token = chosen // TOP
        rows_x = jnp.where(is_valid[:, None], tokens[owner_token], jnp.zeros((), tokens.dtype))
        rows_dy = jnp.where(is_valid[:, None], cotangent[owner_token], jnp.zeros((), cotangent.dtype))
        rows_gate = jnp.where(is_valid, flat_gates[chosen], jnp.zeros((), gates.dtype))
        results = expert_rows(rows_x, rows_dy, rows_gate, w_gate[expert], w_up[expert], w_down[expert])
        input_total = input_total.at[owner_token].add(jnp.where(is_valid[:, None], results[0].astype(jnp.float32), jnp.float32(0.0)))
        gate_total = gate_total.at[chosen].add(jnp.where(is_valid, results[1].astype(jnp.float32), jnp.float32(0.0)))
        return (input_total, gate_total), (results[2], results[3], results[4])

    start_state = (jnp.zeros((TOKENS, D), jnp.float32), jnp.zeros((pick_count,), jnp.float32))
    final_state, weight_grads = lax.scan(one_expert, start_state, expert_ids)
    input_grad = final_state[0].astype(jnp.bfloat16)
    gate_grad = final_state[1].reshape(TOKENS, TOP).astype(jnp.bfloat16)
    return input_grad, gate_grad, weight_grads[0], weight_grads[1], weight_grads[2]
```

```python
import jax
import jax.numpy as jnp
from jax import lax
from jax.sharding import PartitionSpec as P

EXPERT_AXES = ("node", "local")
PIECE_TOKENS = 2048


def local(tokens, cotangent, routes, gates, w_gate, w_up, w_down):
    tokens_dev, width = tokens.shape
    half, units = w_gate.shape[1:]
    members = lax.axis_size("local")
    experts = lax.axis_size("node") * members
    replicas = lax.axis_size("dp")
    expert = lax.axis_index("node") * members + lax.axis_index("local")
    dp = lax.axis_index("dp")

    named = routes[:, :, None] == jnp.arange(experts, dtype=jnp.int32)[None, None, :]
    table = jnp.sum(
        jnp.where(named, gates.astype(jnp.float32)[:, :, None], 0.0), axis=1
    ).astype(jnp.bfloat16)

    w_in = lax.all_gather(
        jnp.concatenate([w_gate[0], w_up[0]], axis=1), "dp", axis=0, tiled=True
    )
    w_out = lax.all_gather(w_down[0], "dp", axis=0, tiled=True)
    mine = jnp.arange(experts, dtype=jnp.int32)[None, :] == expert
    over_rows = (((0,), (0,)), ((), ()))

    def piece(tokens, cotangent, table):
        all_table = lax.all_gather(table, EXPERT_AXES, axis=0, tiled=True)
        x = lax.all_gather(tokens, EXPERT_AXES, axis=0, tiled=True)
        dy = lax.all_gather(cotangent, EXPERT_AXES, axis=0, tiled=True)
        weight = jnp.sum(jnp.where(mine, all_table.astype(jnp.float32), 0.0), axis=1)[:, None]
        pre = jnp.dot(x, w_in, preferred_element_type=jnp.float32)
        upstream = jnp.dot(dy, w_out, preferred_element_type=jnp.float32)
        pre_gate, pre_up = pre[:, :units], pre[:, units:]
        sig = jax.nn.sigmoid(pre_gate)
        activated = pre_gate * sig
        hidden = activated * pre_up
        gate_row = jnp.sum(upstream * hidden, axis=1).astype(jnp.bfloat16)
        scaled_hidden = (weight * hidden).astype(jnp.bfloat16)
        hidden_grad = weight * upstream
        gate_part = hidden_grad * pre_up * sig * (1.0 + pre_gate * (1.0 - sig))
        pre_grad = jnp.concatenate(
            [gate_part.astype(jnp.bfloat16), (hidden_grad * activated).astype(jnp.bfloat16)],
            axis=1,
        )
        rows = lax.dot_general(
            pre_grad, w_in, (((1,), (1,)), ((), ())), preferred_element_type=jnp.float32
        ).astype(jnp.bfloat16)
        input_grad = lax.psum_scatter(rows, EXPERT_AXES, scatter_dimension=0, tiled=True)
        in_grad = lax.dot_general(x, pre_grad, over_rows, preferred_element_type=jnp.float32)
        out_grad = lax.dot_general(
            dy, scaled_hidden, over_rows, preferred_element_type=jnp.float32
        )
        gate_rows = lax.all_gather(gate_row, EXPERT_AXES, axis=0, tiled=True)
        count = tokens.shape[0]
        gate_rows = lax.dynamic_slice_in_dim(
            gate_rows.reshape(experts, experts * count), expert * count, count, axis=1
        )
        return in_grad, out_grad, input_grad, gate_rows

    pieces = max(1, experts * tokens_dev // PIECE_TOKENS)
    if pieces == 1:
        in_grad, out_grad, input_grad, by_expert = piece(tokens, cotangent, table)
    else:

        def step(running, item):
            got = piece(*item)
            return (running[0] + got[0], running[1] + got[1]), got[2:]

        start = (
            jnp.zeros((width, 2 * units), jnp.float32),
            jnp.zeros((width, units), jnp.float32),
        )
        cut = [a.reshape(pieces, -1, a.shape[1]) for a in (tokens, cotangent, table)]
        (in_grad, out_grad), (input_grad, by_expert) = lax.scan(step, start, tuple(cut))
        input_grad = input_grad.reshape(tokens_dev, width)
        by_expert = by_expert.transpose(1, 0, 2).reshape(experts, tokens_dev)

    def own(total):
        return lax.dynamic_slice_in_dim(total, dp * half, half, axis=0)

    def over_replicas(total):
        acc = own(total)
        for shift in range(1, replicas):
            to = lax.rem(dp + shift, replicas)
            part = lax.dynamic_slice_in_dim(total, to * half, half, axis=0)
            pairs = [(i, (i + shift) % replicas) for i in range(replicas)]
            acc = acc + lax.ppermute(part.astype(jnp.bfloat16), "dp", pairs).astype(jnp.float32)
        return acc

    in_sum = over_replicas(in_grad)
    out_sum = over_replicas(out_grad)

    gate_grad = jnp.sum(
        jnp.where(named, by_expert.T.astype(jnp.float32)[:, None, :], 0.0), axis=2
    ).astype(jnp.bfloat16)
    return (
        input_grad,
        gate_grad,
        in_sum[:, :units][None],
        in_sum[:, units:][None],
        out_sum[None],
    )


def solution(mesh):
    rows = P(("dp", "node", "local"), None)
    weights = P(("node", "local"), "dp", None)
    return jax.shard_map(
        local,
        mesh=mesh,
        in_specs=(rows, rows, rows, rows, weights, weights, weights),
        out_specs=(rows, rows, weights, weights, weights),
        check_vma=False,
    )
```

```python
import jax
import jax.numpy as jnp
from jax import lax
from jax.sharding import PartitionSpec as P

PIECE_TOKENS = 2048


def local(tokens, cotangent, routes, gates, w_gate, w_up, w_down):
    tokens_dev, width = tokens.shape
    half, units = w_gate.shape[1:]
    members = lax.axis_size("local")
    experts = lax.axis_size("node") * members
    replicas = lax.axis_size("dp")
    expert = lax.axis_index("node") * members + lax.axis_index("local")
    dp = lax.axis_index("dp")

    named = routes[:, :, None] == jnp.arange(experts, dtype=jnp.int32)[None, None, :]
    table = jnp.sum(
        jnp.where(named, gates.astype(jnp.float32)[:, :, None], 0.0), axis=1
    ).astype(jnp.bfloat16)

    def over_dp(shard):
        full = jnp.zeros((replicas * half, shard.shape[1]), shard.dtype)
        full = lax.dynamic_update_slice_in_dim(full, shard, dp * half, axis=0)
        for shift in range(1, replicas):
            pairs = [(i, (i + shift) % replicas) for i in range(replicas)]
            origin = lax.rem(dp + replicas - shift, replicas)
            full = lax.dynamic_update_slice_in_dim(
                full, lax.ppermute(shard, "dp", pairs), origin * half, axis=0
            )
        return full

    w_in = over_dp(jnp.concatenate([w_gate[0], w_up[0]], axis=1))
    w_out = over_dp(w_down[0])
    padded = (experts + 127) // 128 * 128
    table = jnp.pad(table, ((0, 0), (0, padded - experts)))
    order = list(range(0, members, 2)) + list(range(members - 1, 0, -2))
    rightward = [(order[i], order[(i + 1) % members]) for i in range(members)]
    leftward = [(b, a) for a, b in rightward]
    right_steps = members // 2
    left_steps = members - 1 - right_steps
    groups = lax.axis_size("node")

    mine = jnp.arange(padded, dtype=jnp.int32)[None, :] == expert
    over_rows = (((0,), (0,)), ((), ()))

    def work(x, dy, all_table):
        weight = jnp.sum(jnp.where(mine, all_table.astype(jnp.float32), 0.0), axis=1)[:, None]
        pre = jnp.dot(x, w_in, preferred_element_type=jnp.float32)
        upstream = jnp.dot(dy, w_out, preferred_element_type=jnp.float32)
        pre_gate, pre_up = pre[:, :units], pre[:, units:]
        sig = jax.nn.sigmoid(pre_gate)
        activated = pre_gate * sig
        hidden = activated * pre_up
        gate_row = jnp.sum(upstream * hidden, axis=1)[:, None]
        gate_cols = jnp.where(mine, gate_row, 0.0).astype(jnp.bfloat16)
        scaled_hidden = (weight * hidden).astype(jnp.bfloat16)
        hidden_grad = weight * upstream
        gate_part = hidden_grad * pre_up * sig * (1.0 + pre_gate * (1.0 - sig))
        pre_grad = jnp.concatenate(
            [gate_part.astype(jnp.bfloat16), (hidden_grad * activated).astype(jnp.bfloat16)],
            axis=1,
        )
        rows = lax.dot_general(
            pre_grad, w_in, (((1,), (1,)), ((), ())), preferred_element_type=jnp.float32
        ).astype(jnp.bfloat16)
        in_grad = lax.dot_general(x, pre_grad, over_rows, preferred_element_type=jnp.float32)
        out_grad = lax.dot_general(
            dy, scaled_hidden, over_rows, preferred_element_type=jnp.float32
        )
        return in_grad, out_grad, rows, gate_cols

    def piece(tokens, cotangent, table):
        count = tokens.shape[0]
        block = jnp.concatenate([tokens, cotangent, table], axis=1)
        slots = {0: block}
        for step in range(1, right_steps + 1):
            slots[-step] = lax.ppermute(slots[1 - step], "local", rightward)
            if step <= left_steps:
                slots[step] = lax.ppermute(slots[step - 1], "local", leftward)
        near = right_steps // 2
        halves = [
            [k for k in slots if abs(k) <= near],
            [k for k in slots if abs(k) > near],
        ]
        in_grad = out_grad = None
        totals = {}
        for keys in halves:
            if not keys:
                continue
            blocks = [slots[k] for k in keys]
            for g in range(1, groups):
                pairs = [(i, (i + g) % groups) for i in range(groups)]
                blocks += [lax.ppermute(slots[k], "node", pairs) for k in keys]
            got = work(
                jnp.concatenate([b[:, :width] for b in blocks]),
                jnp.concatenate([b[:, width : 2 * width] for b in blocks]),
                jnp.concatenate([b[:, 2 * width :] for b in blocks]),
            )
            in_grad = got[0] if in_grad is None else in_grad + got[0]
            out_grad = got[1] if out_grad is None else out_grad + got[1]
            size = len(keys) * count
            sums = [part[:size].astype(jnp.float32) for part in got[2:]]
            for g in range(1, groups):
                pairs = [(i, (i - g) % groups) for i in range(groups)]
                for n, part in enumerate(got[2:]):
                    back = lax.ppermute(part[g * size : (g + 1) * size], "node", pairs)
                    sums[n] = sums[n] + back.astype(jnp.float32)
            total = jnp.concatenate(sums, axis=1).astype(jnp.bfloat16)
            for n, k in enumerate(keys):
                totals[k] = total[n * count : (n + 1) * count]

        home = totals[0].astype(jnp.float32)
        for far, sign, pairs in ((right_steps, -1, leftward), (left_steps, 1, rightward)):
            if far == 0:
                continue
            moving = totals[sign * far]
            for step in range(far, 1, -1):
                moving = lax.ppermute(moving, "local", pairs).astype(jnp.float32)
                moving = (moving + totals[sign * (step - 1)].astype(jnp.float32)).astype(
                    jnp.bfloat16
                )
            home = home + lax.ppermute(moving, "local", pairs).astype(jnp.float32)
        home = home.astype(jnp.bfloat16)
        return in_grad, out_grad, home[:, :width], home[:, width : width + experts]

    pieces = max(1, experts * tokens_dev // PIECE_TOKENS)
    if pieces == 1:
        in_grad, out_grad, input_grad, by_expert = piece(tokens, cotangent, table)
    else:

        def step(running, item):
            got = piece(*item)
            return (running[0] + got[0], running[1] + got[1]), got[2:]

        start = (
            jnp.zeros((width, 2 * units), jnp.float32),
            jnp.zeros((width, units), jnp.float32),
        )
        cut = [a.reshape(pieces, -1, a.shape[1]) for a in (tokens, cotangent, table)]
        (in_grad, out_grad), (input_grad, by_expert) = lax.scan(step, start, tuple(cut))
        input_grad = input_grad.reshape(tokens_dev, width)
        by_expert = by_expert.reshape(tokens_dev, experts)

    def own(total):
        return lax.dynamic_slice_in_dim(total, dp * half, half, axis=0)

    def over_replicas(total):
        acc = own(total)
        for shift in range(1, replicas):
            to = lax.rem(dp + shift, replicas)
            part = lax.dynamic_slice_in_dim(total, to * half, half, axis=0)
            pairs = [(i, (i + shift) % replicas) for i in range(replicas)]
            acc = acc + lax.ppermute(part.astype(jnp.bfloat16), "dp", pairs).astype(jnp.float32)
        return acc

    in_sum = over_replicas(in_grad)
    out_sum = over_replicas(out_grad)

    gate_grad = jnp.sum(
        jnp.where(named, by_expert.astype(jnp.float32)[:, None, :], 0.0), axis=2
    ).astype(jnp.bfloat16)
    return (
        input_grad,
        gate_grad,
        in_sum[:, :units][None],
        in_sum[:, units:][None],
        out_sum[None],
    )


def solution(mesh):
    rows = P(("dp", "node", "local"), None)
    weights = P(("node", "local"), "dp", None)
    return jax.shard_map(
        local,
        mesh=mesh,
        in_specs=(rows, rows, rows, rows, weights, weights, weights),
        out_specs=(rows, rows, weights, weights, weights),
        check_vma=False,
    )
```
